32 devices in a mesh: inb: 4 (over y, x), hid: 8 (over z, core).
Axes of the slice: x: 2, y: 2, z: 4, core: 2. Of those that a mesh axis runs over, the one named last changes fastest.
Arguments:
- activations: bfloat16 [2, 512, 4096], P(None, 'hid', 'inb'), may hold values from -40 to 40
- out_grads: bfloat16 [2, 512, 8192], P(None, 'inb', 'hid'), may hold values from -1 to 1
- basis_in: bfloat16 [4096, 1024], P('inb', 'hid'), may hold values from -0.1875 to 0.1875
- basis_out: bfloat16 [8192, 1024], P('hid', 'inb'), may hold values from -0.1875 to 0.1875
Outputs:
- precond: bfloat16 [4096, 8192], P('inb', 'hid')
The draws below stay inside these ranges and needn't reach their ends.
All inputs are finite; a program needn't handle non-finite values.
Results may differ from the reference program's by a relative error of at most 0.0058.
Values may be sent and summed in bfloat16 or wider, within the bound.
No kernel may reach another device: no remote copies, remote signals or barrier semaphores. Data moves between devices by JAX's collectives and lax.ppermute only.
A program may use at most 64 MiB of HBM per device.

```python
import math
import jax
import jax.numpy as jnp
from jax import lax

BLOCK = 1024
MICRO = 2
MB_TOK = 512
IN = 4096
HID = 8192


def token_levels(key):
    level = jax.random.uniform(jax.random.fold_in(key, 4242), (MICRO, MB_TOK), jnp.float32)
    return 10.0 ** (level - 0.5)


def draw_activations(key, part):
    row_scale = token_levels(key)
    column_scale = 10.0 ** (jax.random.uniform(jax.random.fold_in(key, 17), (IN,), jnp.float32) - 0.5)
    noise_key = jax.random.fold_in(key, 23)
    noise = jax.random.truncated_normal(noise_key, -4.0, 4.0, (MICRO, MB_TOK, IN), jnp.float32)
    values = noise * row_scale[:, :, None] * column_scale[None, None, :]
    return jnp.clip(values, -40.0, 40.0).astype(jnp.bfloat16)


def draw_out_grads(key, part):
    row_scale = token_levels(key)
    overall = 0.2 / math.sqrt(MICRO * MB_TOK)
    noise_key = jax.random.fold_in(key, 31)
    noise = jax.random.truncated_normal(noise_key, -4.0, 4.0, (MICRO, MB_TOK, HID), jnp.float32)
    values = noise * row_scale[:, :, None] * overall
    return jnp.clip(values, -1.0, 1.0).astype(jnp.bfloat16)


def levels(key, shape, pieces, least, largest):
    loudness = 1.0
    for position, parts in pieces:
        heights = jax.random.uniform(jax.random.fold_in(jax.random.fold_in(key, 6), position), (parts,), jnp.float32, least / len(pieces), largest / len(pieces))
        loudness = loudness * jnp.repeat(jnp.exp(heights), shape[position] // parts).reshape((-1,) + (1,) * (len(shape) - 1 - position))
    return loudness


def gaussian(own_key, extent, spread, most, split=(), held_as=jnp.bfloat16):
    entries = spread * jax.random.normal(own_key, extent, jnp.float32)
    if split:
        entries = entries * levels(own_key, extent, split, -0.22, 0.18)
    return jnp.clip(entries, -most, most).astype(held_as)


def setup_inputs(seed: int = 0) -> dict:
    seeds = jax.random.split(jax.random.key(seed), 5)
    activations = draw_activations(jax.random.fold_in(seeds[4], 71), 0)
    out_grads = draw_out_grads(jax.random.fold_in(seeds[4], 71), 0)
    basis_in = gaussian(seeds[2], (IN, BLOCK), BLOCK ** -0.5, 0.1875, ((0, 4), (1, 8)))
    basis_out = gaussian(seeds[3], (HID, BLOCK), BLOCK ** -0.5, 0.1875, ((0, 8), (1, 4)))
    return {"activations": activations, "out_grads": out_grads, "basis_in": basis_in, "basis_out": basis_out}


damping = 0.1


def rotate_all(values, basis, block_count):
    def rotate_block(number):
        offset = (number * BLOCK).astype(jnp.int32)
        segment = lax.dynamic_slice_in_dim(values, offset, BLOCK, 1)
        square_part = lax.dynamic_slice_in_dim(basis, offset, BLOCK, 0)
        return jnp.dot(segment, square_part, preferred_element_type=jnp.float32).astype(jnp.bfloat16)
    return lax.map(rotate_block, jnp.arange(block_count, dtype=jnp.int32))


def square_round(values):
    widened = values.astype(jnp.float32)
    return (widened * widened).astype(jnp.bfloat16)


def reference(activations, out_grads, basis_in, basis_out):
    total_tokens = MICRO * MB_TOK
    acts_flat = activations.reshape(total_tokens, IN)
    grads_flat = out_grads.reshape(total_tokens, HID)
    rot_in = rotate_all(acts_flat, basis_in, IN // BLOCK)
    rot_out = rotate_all(grads_flat, basis_out, HID // BLOCK)
    grad_rows = jnp.transpose(rot_out, (1, 0, 2)).reshape(total_tokens, HID)
    grad_squares = square_round(grad_rows)
    dims = (((0,), (0,)), ((), ()))

    def tile_rows(act_rot):
        act_squares = square_round(act_rot)
        grad_rot = lax.dot_general(act_rot, grad_rows, dims, preferred_element_type=jnp.float32)
        fisher = lax.dot_general(act_squares, grad_squares, dims, preferred_element_type=jnp.float32)
        return (grad_rot / (fisher + damping)).astype(jnp.bfloat16)

    tiles = lax.map(tile_rows, rot_in)
    return tiles.reshape(IN, HID)
```

```python
import jax
import jax.numpy as jnp
from jax import lax
from jax.experimental import pallas as pl
from jax.experimental.pallas import tpu as pltpu
from jax.sharding import PartitionSpec as P

damping = 0.1


def square_round(values):
    widened = values.astype(jnp.float32)
    return (widened * widened).astype(jnp.bfloat16)


def contract_tokens(left_side, right_side):
    return lax.dot_general(
        left_side, right_side, (((0, 1), (0, 1)), ((), ())), preferred_element_type=jnp.float32
    )


def gathered(activations, out_grads, basis_in, basis_out):
    width_block = basis_in.shape[0]
    grads_flat = out_grads.reshape(-1, width_block)
    grads_rot = (
        jnp.dot(
            grads_flat,
            lax.all_gather(basis_out, "inb", axis=1, tiled=True),
            preferred_element_type=jnp.float32,
        )
        .astype(jnp.bfloat16)
        .reshape(out_grads.shape)
    )
    basis_whole = lax.all_gather(basis_in, "hid", axis=1, tiled=True)
    grads_full = lax.all_gather(grads_rot, "inb", axis=1, tiled=True)
    grads_squared = square_round(grads_full)
    plain_rows = lax.all_gather(activations, "hid", axis=1, tiled=True)
    rotated = (
        jnp.dot(
            plain_rows.reshape(-1, width_block), basis_whole, preferred_element_type=jnp.float32
        )
        .astype(jnp.bfloat16)
        .reshape(plain_rows.shape)
    )
    grad_sum = contract_tokens(rotated, grads_full)
    fisher_sum = contract_tokens(square_round(rotated), grads_squared)
    return (grad_sum / (fisher_sum + damping)).astype(jnp.bfloat16)


def swap(values, axis, count, distance):
    return lax.ppermute(values, axis, [(i, i ^ distance) for i in range(count)])


def rows_of(index, size):
    return pl.ds(pl.multiple_of(index * size, size), size)


def rotate_out_kernel(run, own_ref, near_ref, basis_ref, far_ref, tile_ref):
    index = lax.axis_index("inb")
    low, high = lax.rem(index, 2), index // 2
    micro, tokens, depth = own_ref.shape
    width = basis_ref.shape[1]
    for grads_ref, place in ((own_ref, low), (near_ref, 1 - low)):
        grads = grads_ref[...].reshape(micro * tokens, depth)
        for weights_ref, column in ((basis_ref, high), (far_ref, 1 - high)):
            part = jnp.dot(grads, weights_ref[...], preferred_element_type=jnp.float32)
            part = part.astype(jnp.bfloat16)
            for m in range(micro):
                for k in range(tokens // run):
                    here = m * tokens + k * run
                    row = place * (micro * tokens) + (k * micro + m) * run
                    tile_ref[
                        pl.ds(pl.multiple_of(row, run), run), rows_of(column, width)
                    ] = part[here : here + run]


def rotate_in_kernel(own_ref, core_ref, near_ref, near_core_ref, basis_ref, far_ref, tile_ref, weights):
    index = lax.axis_index("hid")
    core, low, high = lax.rem(index, 2), lax.rem(index // 2, 2), index // 4
    micro, tokens, depth = own_ref.shape
    width = basis_ref.shape[1]
    weights[:, rows_of(high, width)] = basis_ref[...]
    weights[:, rows_of(1 - high, width)] = far_ref[...]
    for acts_ref, place in (
        (own_ref, 2 * low + core),
        (core_ref, 2 * low + 1 - core),
        (near_ref, 2 * (1 - low) + core),
        (near_core_ref, 2 * (1 - low) + 1 - core),
    ):
        acts = acts_ref[...].reshape(micro * tokens, depth)
        part = jnp.dot(acts, weights[...], preferred_element_type=jnp.float32)
        tile_ref[:, rows_of(place, micro * tokens)] = part.astype(jnp.bfloat16).T


def final_kernel(
    t0, t1, t2, t3, t4, s0, s1, s2, s3, g0, g1, g2, g3, out_ref, left, right, right_squared
):
    @pl.when(pl.program_id(0) == 0)
    def _():
        index = lax.axis_index("hid")
        core, low, high = lax.rem(index, 2), lax.rem(index // 2, 2), index // 4
        width, span = t0.shape[0] // 2, t0.shape[1]
        inner = low != high
        t3_value = jnp.where(inner, t3[...], t4[...])
        for piece, dl, dh, dc in (
            (t0[...], 0, 0, 0), (t1[...], 1, 0, 0), (t2[...], 0, 1, 0), (t3_value, 1, 1, 0),
            (s0[...], 0, 0, 1), (s1[...], 1, 0, 1), (s2[...], 0, 1, 1), (s3[...], 1, 1, 1),
        ):
            piece_low = low if dl == 0 else 1 - low
            piece_high = high if dh == 0 else 1 - high
            piece_core = core if dc == 0 else 1 - core
            for k in range(2):
                row = 4 * k + 2 * piece_low + piece_core
                left[rows_of(row, width), rows_of(piece_high, span)] = piece[k * width : (k + 1) * width]
        index = lax.axis_index("inb")
        low, high = lax.rem(index, 2), index // 2
        span, width = g0.shape[0], g0.shape[1] // 2
        for piece, dl, dh in ((g0, 0, 0), (g1, 1, 0), (g2, 0, 1), (g3, 1, 1)):
            piece_low = low if dl == 0 else 1 - low
            piece_high = high if dh == 0 else 1 - high
            for k in range(2):
                values = piece[:, k * width : (k + 1) * width]
                at = (rows_of(piece_high, span), rows_of(2 * k + piece_low, width))
                right[at] = values
                right_squared[at] = values * values

    block = out_ref.shape[0]
    rows = left[rows_of(pl.program_id(0), block), :]
    grad = jnp.dot(rows, right[...], preferred_element_type=jnp.float32)
    fisher = jnp.dot(rows * rows, right_squared[...], preferred_element_type=jnp.float32)
    out_ref[...] = (grad / (fisher + damping)).astype(jnp.bfloat16)


def paired(n_inb, n_hid, activations, out_grads, basis_in, basis_out):
    vmem = pl.BlockSpec(memory_space=pltpu.VMEM)
    params = pltpu.CompilerParams(vmem_limit_bytes=40 * 1024 * 1024)
    low_in, high_in = n_hid // 4, n_hid // 2
    low_out, high_out = n_inb // 4, n_inb // 2

    def hid(values, distance):
        return swap(values, "hid", n_hid, distance)

    def inb(values, distance):
        return swap(values, "inb", n_inb, distance)

    acts_core = hid(activations, 1)
    basis_far = hid(basis_in, high_in)
    acts_near = hid(activations, low_in)
    grads_near = inb(out_grads, low_out)
    basis_out_far = inb(basis_out, high_out)
    acts_near_core = hid(acts_near, 1)

    micro, tin, _ = activations.shape
    tout = out_grads.shape[1]
    t0 = pl.pallas_call(
        rotate_in_kernel,
        out_shape=jax.ShapeDtypeStruct((2 * basis_in.shape[1], 4 * micro * tin), jnp.bfloat16),
        in_specs=[vmem] * 6,
        out_specs=vmem,
        scratch_shapes=[pltpu.VMEM((basis_in.shape[0], 2 * basis_in.shape[1]), jnp.bfloat16)],
        compiler_params=params,
    )(activations, acts_core, acts_near, acts_near_core, basis_in, basis_far)
    g0 = pl.pallas_call(
        lambda *refs: rotate_out_kernel(tin, *refs),
        out_shape=jax.ShapeDtypeStruct((2 * micro * tout, 2 * basis_out.shape[1]), jnp.bfloat16),
        in_specs=[vmem] * 4,
        out_specs=vmem,
        compiler_params=params,
    )(out_grads, grads_near, basis_out, basis_out_far)

    t2 = hid(t0, high_in)
    t1 = hid(t0, low_in)
    g1 = inb(g0, low_out)
    g2 = inb(g0, high_out)
    s0 = hid(t0, 1)
    s1 = hid(t1, 1)
    s2 = hid(t2, 1)
    chips = n_hid // 2
    inner = [(2 * z + c, 2 * (chips - 1 - z) + c) for z in range(1, chips - 1) for c in range(2)]
    outer = [(2 * z + c, 2 * (z ^ 1) + c) for z in range(1, chips - 1) for c in range(2)]
    t3 = lax.ppermute(t0, "hid", inner)
    t4 = lax.ppermute(t2, "hid", outer)
    core = lax.rem(lax.axis_index("hid"), 2)
    onward = []
    for h in range(n_hid):
        step = high_out if h % 2 == 0 else low_out
        onward += [(i * n_hid + h, (i ^ step) * n_hid + h) for i in range(n_inb)]
    g3 = lax.ppermute(jnp.where(core == 0, g1, g2), ("inb", "hid"), onward)
    zone = lax.axis_index("hid") // 2
    is_inner = (zone > 0) & (zone < chips - 1)
    s3 = hid(jnp.where(is_inner, t3, t4), 1)

    rows, columns = activations.shape[2], out_grads.shape[2]
    steps = 4
    whole = lambda v: pl.BlockSpec(v.shape, lambda r: (0, 0))
    pieces = (t0, t1, t2, t3, t4, s0, s1, s2, s3, g0, g1, g2, g3)
    total = t0.shape[1] * 2
    return pl.pallas_call(
        final_kernel,
        grid=(steps,),
        out_shape=jax.ShapeDtypeStruct((rows, columns), jnp.bfloat16),
        in_specs=[vmem for v in pieces],
        out_specs=pl.BlockSpec((rows // steps, columns), lambda r: (r, 0)),
        scratch_shapes=[
            pltpu.VMEM((rows, total), jnp.bfloat16),
            pltpu.VMEM((total, columns), jnp.bfloat16),
            pltpu.VMEM((total, columns), jnp.bfloat16),
        ],
        compiler_params=params,
    )(*pieces)


def solution(mesh):
    n_inb, n_hid = mesh.shape["inb"], mesh.shape["hid"]
    two_by_two = n_inb == 2 * 2 and n_hid == 2 * n_inb
    body = (lambda *a: paired(n_inb, n_hid, *a)) if two_by_two else gathered
    return jax.shard_map(
        body,
        mesh=mesh,
        in_specs=(P(None, "hid", "inb"), P(None, "inb", "hid"), P("inb", "hid"), P("hid", "inb")),
        out_specs=P("inb", "hid"),
        check_vma=False,
    )
```

```python
import jax
import jax.numpy as jnp
from jax import lax
from jax.experimental import pallas as pl
from jax.experimental.pallas import tpu as pltpu
from jax.sharding import PartitionSpec as P

damping = 0.1


def square_round(values):
    widened = values.astype(jnp.float32)
    return (widened * widened).astype(jnp.bfloat16)


def contract_tokens(left_side, right_side):
    return lax.dot_general(
        left_side, right_side, (((0, 1), (0, 1)), ((), ())), preferred_element_type=jnp.float32
    )


def gathered(activations, out_grads, basis_in, basis_out):
    width_block = basis_in.shape[0]
    grads_flat = out_grads.reshape(-1, width_block)
    grads_rot = (
        jnp.dot(
            grads_flat,
            lax.all_gather(basis_out, "inb", axis=1, tiled=True),
            preferred_element_type=jnp.float32,
        )
        .astype(jnp.bfloat16)
        .reshape(out_grads.shape)
    )
    basis_whole = lax.all_gather(basis_in, "hid", axis=1, tiled=True)
    grads_full = lax.all_gather(grads_rot, "inb", axis=1, tiled=True)
    grads_squared = square_round(grads_full)
    plain_rows = lax.all_gather(activations, "hid", axis=1, tiled=True)
    rotated = (
        jnp.dot(
            plain_rows.reshape(-1, width_block), basis_whole, preferred_element_type=jnp.float32
        )
        .astype(jnp.bfloat16)
        .reshape(plain_rows.shape)
    )
    grad_sum = contract_tokens(rotated, grads_full)
    fisher_sum = contract_tokens(square_round(rotated), grads_squared)
    return (grad_sum / (fisher_sum + damping)).astype(jnp.bfloat16)


def swap(values, axis, count, distance):
    return lax.ppermute(values, axis, [(i, i ^ distance) for i in range(count)])


def rows_of(index, size):
    return pl.ds(pl.multiple_of(index * size, size), size)


def hid_digits():
    index = lax.axis_index("hid")
    return index // 4, lax.rem(index // 2, 2), lax.rem(index, 2)


def inb_digits():
    index = lax.axis_index("inb")
    return index // 2, lax.rem(index, 2)


def other_tokens():
    return lax.rem(hid_digits()[1] + inb_digits()[1], 2)


def dot(a, b):
    return jnp.dot(a, b, preferred_element_type=jnp.float32)


def fetch_kernel(*refs):
    count = len(refs) // 2
    copies = [pltpu.make_async_copy(refs[k], refs[count + k], refs[-1].at[k]) for k in range(count)]
    for copy in copies:
        copy.start()
    for copy in copies:
        copy.wait()


def rotate_out_kernel(run, own_ref, near_ref, basis_ref, far_ref, tile_ref, weights):
    tok, col = inb_digits()
    micro, tokens, depth = own_ref.shape
    width = basis_ref.shape[1]
    weights[:, rows_of(col, width)] = basis_ref[...]
    weights[:, rows_of(1 - col, width)] = far_ref[...]
    for grads_ref, place in ((own_ref, tok), (near_ref, 1 - tok)):
        part = dot(grads_ref[...].reshape(micro * tokens, depth), weights[...]).astype(jnp.bfloat16)
        for m in range(micro):
            for k in range(tokens // run):
                here = m * tokens + k * run
                row = place * (micro * tokens) + (k * micro + m) * run
                tile_ref[pl.ds(pl.multiple_of(row, run), run), :] = part[here : here + run]


def join_kernel(basis_ref, far_ref, weights):
    col = hid_digits()[1]
    width = basis_ref.shape[1]
    weights[:, rows_of(col, width)] = basis_ref[...]
    weights[:, rows_of(1 - col, width)] = far_ref[...]


def rotate_in_kernel(own_ref, core_ref, near_ref, near_core_ref, weights, tile_ref):
    tok, _, core = hid_digits()
    micro, tokens, depth = own_ref.shape
    for acts_ref, place in (
        (own_ref, 2 * tok + core),
        (core_ref, 2 * tok + 1 - core),
        (near_ref, 2 * (1 - tok) + core),
        (near_core_ref, 2 * (1 - tok) + 1 - core),
    ):
        acts = acts_ref[...].reshape(micro * tokens, depth)
        part = dot(acts, weights[...])
        tile_ref[:, rows_of(place, micro * tokens)] = part.astype(jnp.bfloat16).T


def pick_kernel(which, a_ref, b_ref, out_ref):
    first = which()

    @pl.when(first)
    def _():
        out_ref[...] = a_ref[...]

    @pl.when(jnp.logical_not(first))
    def _():
        out_ref[...] = b_ref[...]


def copy_kernel(a_ref, out_ref):
    out_ref[...] = a_ref[...]


def is_first_core():
    return hid_digits()[2] == 0


def is_inner_chip():
    tok, col, _ = hid_digits()
    return tok != col


def early_kernel(t0, t1, t2, s0, s1, s2, g0, g1, g2, ready, grad, fisher, left, right, side):
    other = other_tokens()
    size, span = t0.shape
    for k, (t, t_far, t_side) in enumerate(((t0, t2, t1), (s0, s2, s1))):
        at = slice(k * size, (k + 1) * size)
        left[at, :span] = t[...]
        left[at, span:] = t_far[...]
        side[at] = t_side[...]
    right[rows_of(other, span), :] = g0[...]
    right[rows_of(1 - other, span), :] = g2[...]
    whole, below = right[...], g1[...]
    whole_squared, below_squared = whole * whole, below * below
    for k in range(2):
        at = slice(k * size, (k + 1) * size)
        rows = left[at]
        g = dot(rows, whole)
        f = dot(rows * rows, whole_squared)
        ready[at] = (g / (f + damping)).astype(jnp.bfloat16)
        rows = left[at, rows_of(other, span)]
        grad[0, at] = dot(rows, below)
        fisher[0, at] = dot(rows * rows, below_squared)
        rows = side[at]
        grad[1, at] = dot(rows, whole[:span])
        fisher[1, at] = dot(rows * rows, whole_squared[:span])

    @pl.when(other == 0)
    def _():
        for k in range(2):
            at = slice(k * size, (k + 1) * size)
            rows = side[at]
            grad[2, at] = dot(rows, below)
            fisher[2, at] = dot(rows * rows, below_squared)


def late_kernel(ready, grad, fisher, left, right, side, g1, t3, s3, g3, out_ref, done, sems):
    tok, col, core = hid_digits()
    out_tok, _ = inb_digits()
    other = other_tokens()
    size, span = t3.shape
    row_size, width = size // 2, ready.shape[1]
    copies = []

    def send(quadrant, part, source, row_tok, column_tok):
        for k in range(2):
            row = 4 * row_tok + 2 * k + (core if part == 0 else 1 - core)
            copy = pltpu.make_async_copy(
                source.at[pl.ds(part * size + k * row_size, row_size), :],
                out_ref.at[rows_of(row, row_size), rows_of(column_tok, width)],
                sems.at[4 * quadrant + 2 * part + k],
            )
            copy.start()
            copies.append(copy)

    def divided(quadrant, at, g, f):
        done[quadrant, at] = (g / (f + damping)).astype(jnp.bfloat16)

    for part in range(2):
        send(3, part, ready, tok, out_tok)
    below, beside = g3[...], right[span:]
    below_squared, beside_squared = below * below, beside * beside
    parts = [(slice(k * size, (k + 1) * size), k, t) for k, t in enumerate((t3, s3))]
    for at, k, _ in parts:
        rows = left[at, rows_of(1 - other, span)]
        divided(0, at, grad[0, at] + dot(rows, below), fisher[0, at] + dot(rows * rows, below_squared))
        send(0, k, done.at[0], tok, 1 - out_tok)
    for at, k, t in parts:
        rows = t[...]
        divided(1, at, grad[1, at] + dot(rows, beside), fisher[1, at] + dot(rows * rows, beside_squared))
        send(1, k, done.at[1], 1 - tok, out_tok)

    @pl.when(other == 0)
    def _():
        for at, _, t in parts:
            rows = t[...]
            divided(2, at, grad[2, at] + dot(rows, below), fisher[2, at] + dot(rows * rows, below_squared))

    @pl.when(other == 1)
    def _():
        last = g1[...]
        last_squared = last * last
        for at, _, t in parts:
            rows, near = t[...], side[at]
            g = dot(rows, last) + dot(near, below)
            f = dot(rows * rows, last_squared) + dot(near * near, below_squared)
            divided(2, at, g, f)

    for part in range(2):
        send(2, part, done.at[2], 1 - tok, 1 - out_tok)
    for copy in copies:
        copy.wait()


def paired(n_inb, n_hid, activations, out_grads, basis_in, basis_out):
    vmem, anywhere = pl.BlockSpec(memory_space=pltpu.VMEM), pl.BlockSpec(memory_space=pl.ANY)
    params = pltpu.CompilerParams(vmem_limit_bytes=24 * 1024 * 1024)
    bf16, f32 = jnp.bfloat16, jnp.float32
    shape = jax.ShapeDtypeStruct

    def hid(values, distance):
        return swap(values, "hid", n_hid, distance)

    def inb(values, distance):
        return swap(values, "inb", n_inb, distance)

    tok_in, col_in = n_hid // 2, n_hid // 4
    tok_out, col_out = n_inb // 2, n_inb // 4

    def call(kernel, outs, operands, scratch=(), flops=0, space=vmem, out_space=vmem):
        one = not isinstance(outs, list)
        return pl.pallas_call(
            kernel,
            out_shape=outs,
            in_specs=[space] * len(operands),
            out_specs=out_space if one else [out_space] * len(outs),
            scratch_shapes=scratch,
            compiler_params=params,
            cost_estimate=pl.CostEstimate(flops=flops, bytes_accessed=0, transcendentals=0),
        )(*operands)

    acts_near = hid(activations, tok_in)
    basis_far = hid(basis_in, col_in)
    grads_near = inb(out_grads, tok_out)
    basis_out_far = inb(basis_out, col_out)
    acts_core = hid(activations, 1)

    own = (out_grads, basis_out, activations, basis_in)
    own_grads, own_basis_out, own_acts, own_basis_in = call(
        fetch_kernel,
        [shape(v.shape, v.dtype) for v in own],
        own,
        [pltpu.SemaphoreType.DMA((len(own),))],
        space=anywhere,
    )
    acts_near, own_acts, own_grads = lax.optimization_barrier((acts_near, own_acts, own_grads))
    acts_near_core = hid(acts_near, 1)

    micro, tin, depth = activations.shape
    tout = out_grads.shape[1]
    rows_out, width_out = micro * tout, basis_out.shape[1]
    rows_in, width_in = micro * tin, basis_in.shape[1]
    tile_in, tile_out = (2 * width_in, 4 * rows_in), (2 * rows_out, 2 * width_out)
    weights = call(join_kernel, shape((depth, 2 * width_in), bf16), (own_basis_in, basis_far), flops=4000000000)
    t0 = call(
        rotate_in_kernel,
        shape(tile_in, bf16),
        (own_acts, acts_core, acts_near, acts_near_core, weights),
        flops=16 * rows_in * width_in * depth,
    )
    grads_near, basis_out_far, t0 = lax.optimization_barrier((grads_near, basis_out_far, t0))
    g0 = call(
        lambda *refs: rotate_out_kernel(tin, *refs),
        shape(tile_out, bf16),
        (own_grads, grads_near, own_basis_out, basis_out_far),
        [pltpu.VMEM((depth, 2 * width_out), bf16)],
        flops=8 * rows_out * width_out * depth,
    )
    t1 = hid(t0, tok_in)
    t2 = hid(t0, col_in)
    g1 = inb(g0, tok_out)
    g2 = inb(g0, col_out)
    s0 = hid(t0, 1)
    s1 = hid(t1, 1)
    s2 = hid(t2, 1)
    chips = n_hid // 2
    ends = (0, chips - 1)
    inner = [(2 * z + c, 2 * (z if z in ends else chips - 1 - z) + c) for z in range(chips) for c in range(2)]
    t4 = hid(call(copy_kernel, shape(tile_in, bf16), (t1,), flops=4000000000), col_in)
    t0_then, _, g1, g2 = lax.optimization_barrier((t0, t1, g1, g2))
    t3 = lax.ppermute(t0_then, "hid", inner)
    onward = []
    for h in range(n_hid):
        step = col_out if h % 2 == 0 else tok_out
        onward += [(i * n_hid + h, (i ^ step) * n_hid + h) for i in range(n_inb)]
    picked = call(lambda *refs: pick_kernel(is_first_core, *refs), shape(tile_out, bf16), (g1, g2))
    g3 = lax.ppermute(picked, ("inb", "hid"), onward)

    half_rows, half_columns, half_tokens = 2 * tile_in[0], tile_out[1], tile_out[0]
    quarter = (half_rows, half_columns)
    ready, grad, fisher, left, right, side = call(
        early_kernel,
        [
            shape(quarter, bf16),
            shape((3,) + quarter, f32),
            shape((3,) + quarter, f32),
            shape((half_rows, 2 * half_tokens), bf16),
            shape((2 * half_tokens, half_columns), bf16),
            shape((half_rows, half_tokens), bf16),
        ],
        (t0, t1, t2, s0, s1, s2, g0, g1, g2),
        flops=20 * half_rows * half_columns * half_tokens,
    )
    t3, t4, ready = lax.optimization_barrier((t3, t4, ready))
    t3 = call(lambda *refs: pick_kernel(is_inner_chip, *refs), shape(tile_in, bf16), (t3, t4))
    s3 = hid(t3, 1)
    operands = (ready, grad, fisher, left, right, side, g1, t3, s3, g3)
    return call(
        late_kernel,
        shape((activations.shape[2], out_grads.shape[2]), bf16),
        operands,
        [pltpu.VMEM((3,) + quarter, bf16), pltpu.SemaphoreType.DMA((16,))],
        flops=16 * half_rows * half_columns * half_tokens,
        out_space=anywhere,
    )


def solution(mesh):
    n_inb, n_hid = mesh.shape["inb"], mesh.shape["hid"]
    two_by_two = n_inb == 2 * 2 and n_hid == 2 * n_inb
    body = (lambda *a: paired(n_inb, n_hid, *a)) if two_by_two else gathered
    return jax.shard_map(
        body,
        mesh=mesh,
        in_specs=(P(None, "hid", "inb"), P(None, "inb", "hid"), P("inb", "hid"), P("hid", "inb")),
        out_specs=P("inb", "hid"),
        check_vma=False,
    )
```

```python
import jax
import jax.numpy as jnp
from jax import lax
from jax.experimental import pallas as pl
from jax.experimental.pallas import tpu as pltpu
from jax.sharding import PartitionSpec as P

damping = 0.1


def square_round(values):
    widened = values.astype(jnp.float32)
    return (widened * widened).astype(jnp.bfloat16)


def contract_tokens(left_side, right_side):
    return lax.dot_general(
        left_side, right_side, (((0, 1), (0, 1)), ((), ())), preferred_element_type=jnp.float32
    )


def gathered(activations, out_grads, basis_in, basis_out):
    width_block = basis_in.shape[0]
    grads_flat = out_grads.reshape(-1, width_block)
    grads_rot = (
        jnp.dot(
            grads_flat,
            lax.all_gather(basis_out, "inb", axis=1, tiled=True),
            preferred_element_type=jnp.float32,
        )
        .astype(jnp.bfloat16)
        .reshape(out_grads.shape)
    )
    basis_whole = lax.all_gather(basis_in, "hid", axis=1, tiled=True)
    grads_full = lax.all_gather(grads_rot, "inb", axis=1, tiled=True)
    grads_squared = square_round(grads_full)
    plain_rows = lax.all_gather(activations, "hid", axis=1, tiled=True)
    rotated = (
        jnp.dot(
            plain_rows.reshape(-1, width_block), basis_whole, preferred_element_type=jnp.float32
        )
        .astype(jnp.bfloat16)
        .reshape(plain_rows.shape)
    )
    grad_sum = contract_tokens(rotated, grads_full)
    fisher_sum = contract_tokens(square_round(rotated), grads_squared)
    return (grad_sum / (fisher_sum + damping)).astype(jnp.bfloat16)


def swap(values, axis, count, distance):
    return lax.ppermute(values, axis, [(i, i ^ distance) for i in range(count)])


def rows_of(index, size):
    return pl.ds(pl.multiple_of(index * size, size), size)


def hid_digits():
    index = lax.axis_index("hid")
    return index // 4, lax.rem(index // 2, 2), lax.rem(index, 2)


def inb_digits():
    index = lax.axis_index("inb")
    return index // 2, lax.rem(index, 2)


def other_tokens():
    return lax.rem(hid_digits()[1] + inb_digits()[1], 2)


def dot(a, b):
    return jnp.dot(a, b, preferred_element_type=jnp.float32)


def fetch_kernel(*refs):
    count = len(refs) // 2
    copies = [pltpu.make_async_copy(refs[k], refs[count + k], refs[-1].at[k]) for k in range(count)]
    for copy in copies:
        copy.start()
    for copy in copies:
        copy.wait()


def rotate_out_kernel(run, own_ref, near_ref, basis_ref, far_ref, tile_ref, weights):
    tok, col = inb_digits()
    micro, tokens, depth = own_ref.shape
    width = basis_ref.shape[1]
    weights[:, rows_of(col, width)] = basis_ref[...]
    weights[:, rows_of(1 - col, width)] = far_ref[...]
    for grads_ref, place in ((own_ref, tok), (near_ref, 1 - tok)):
        part = dot(grads_ref[...].reshape(micro * tokens, depth), weights[...]).astype(jnp.bfloat16)
        for m in range(micro):
            for k in range(tokens // run):
                here = m * tokens + k * run
                row = place * (micro * tokens) + (k * micro + m) * run
                tile_ref[pl.ds(pl.multiple_of(row, run), run), :] = part[here : here + run]


def join_kernel(basis_ref, far_ref, weights):
    col = hid_digits()[1]
    width = basis_ref.shape[1]
    weights[:, rows_of(col, width)] = basis_ref[...]
    weights[:, rows_of(1 - col, width)] = far_ref[...]


def rotate_in_kernel(own_ref, core_ref, near_ref, near_core_ref, weights, tile_ref):
    tok, _, core = hid_digits()
    micro, tokens, depth = own_ref.shape
    for acts_ref, place in (
        (own_ref, 2 * tok + core),
        (core_ref, 2 * tok + 1 - core),
        (near_ref, 2 * (1 - tok) + core),
        (near_core_ref, 2 * (1 - tok) + 1 - core),
    ):
        acts = acts_ref[...].reshape(micro * tokens, depth)
        part = dot(acts, weights[...])
        tile_ref[:, rows_of(place, micro * tokens)] = part.astype(jnp.bfloat16).T


def pick_kernel(which, a_ref, b_ref, out_ref):
    first = which()

    @pl.when(first)
    def _():
        out_ref[...] = a_ref[...]

    @pl.when(jnp.logical_not(first))
    def _():
        out_ref[...] = b_ref[...]


def copy_kernel(a_ref, out_ref):
    out_ref[...] = a_ref[...]


def is_first_core():
    return hid_digits()[2] == 0


def squared(values):
    return values * values


def ratio(g, f):
    return (g / (f + damping)).astype(jnp.bfloat16)


def early_kernel(t0, t1, t2, s0, s1, s2, g0, g1, g2, g3, top, grad, fisher, left, right, side):
    out_tok, _ = inb_digits()
    other = other_tokens()
    size, span = t0.shape
    width = g0.shape[1]
    for k, (t, t_far, t_side) in enumerate(((t0, t2, t1), (s0, s2, s1))):
        at = slice(k * size, (k + 1) * size)
        left[at, :span] = t[...]
        left[at, span:] = t_far[...]
        side[at] = t_side[...]
    for half, column, tile in ((other, out_tok, g0), (1 - other, out_tok, g2), (other, 1 - out_tok, g1), (1 - other, 1 - out_tok, g3)):
        right[rows_of(half, span), rows_of(column, width)] = tile[...]
    for c in range(2):
        columns = slice(c * width, (c + 1) * width)
        whole = right[:, columns]
        whole_squared = squared(whole)
        for k in range(2):
            at = slice(k * size, (k + 1) * size)
            rows = left[at]
            top[at, columns] = ratio(dot(rows, whole), dot(squared(rows), whole_squared))
            rows = side[at]
            grad[at, columns] = dot(rows, whole[:span])
            fisher[at, columns] = dot(squared(rows), whole_squared[:span])


def late_kernel(top, grad, fisher, right, t3, s3, out_ref, done, sems):
    tok, _, core = hid_digits()
    size, span = t3.shape
    row_size, width = size // 2, right.shape[1] // 2
    copies = []

    def send(part, source, row_tok, number):
        for k in range(2):
            row = 4 * row_tok + 2 * k + (core if part == 0 else 1 - core)
            copy = pltpu.make_async_copy(
                source.at[pl.ds(part * size + k * row_size, row_size), :],
                out_ref.at[rows_of(row, row_size), :],
                sems.at[number + k],
            )
            copy.start()
            copies.append(copy)

    for part in range(2):
        send(part, top, tok, 2 * part)
    for part, t in enumerate((t3, s3)):
        at = slice(part * size, (part + 1) * size)
        rows = t[...]
        rows_squared = squared(rows)
        for c in range(2):
            columns = slice(c * width, (c + 1) * width)
            beside = right[span:, columns]
            g = grad[at, columns] + dot(rows, beside)
            f = fisher[at, columns] + dot(rows_squared, squared(beside))
            done[at, columns] = ratio(g, f)
        send(part, done, 1 - tok, 4 + 2 * part)
    for copy in copies:
        copy.wait()


def paired(n_inb, n_hid, activations, out_grads, basis_in, basis_out):
    vmem, anywhere = pl.BlockSpec(memory_space=pltpu.VMEM), pl.BlockSpec(memory_space=pl.ANY)
    params = pltpu.CompilerParams(vmem_limit_bytes=24 * 1024 * 1024)
    bf16, f32 = jnp.bfloat16, jnp.float32
    shape = jax.ShapeDtypeStruct

    def hid(values, distance):
        return swap(values, "hid", n_hid, distance)

    def inb(values, distance):
        return swap(values, "inb", n_inb, distance)

    tok_in, col_in = n_hid // 2, n_hid // 4
    tok_out, col_out = n_inb // 2, n_inb // 4

    def call(kernel, outs, operands, scratch=(), flops=0, space=vmem, out_space=vmem):
        one = not isinstance(outs, list)
        return pl.pallas_call(
            kernel,
            out_shape=outs,
            in_specs=[space] * len(operands),
            out_specs=out_space if one else [out_space] * len(outs),
            scratch_shapes=scratch,
            compiler_params=params,
            cost_estimate=pl.CostEstimate(flops=flops, bytes_accessed=0, transcendentals=0),
        )(*operands)

    acts_near = hid(activations, tok_in)
    basis_far = hid(basis_in, col_in)
    grads_near = inb(out_grads, tok_out)
    basis_out_far = inb(basis_out, col_out)
    acts_core = hid(activations, 1)

    own = (out_grads, basis_out, activations, basis_in)
    own_grads, own_basis_out, own_acts, own_basis_in = call(
        fetch_kernel,
        [shape(v.shape, v.dtype) for v in own],
        own,
        [pltpu.SemaphoreType.DMA((len(own),))],
        space=anywhere,
    )

    micro, tin, depth = activations.shape
    tout = out_grads.shape[1]
    rows_out, width_out = micro * tout, basis_out.shape[1]
    rows_in, width_in = micro * tin, basis_in.shape[1]
    tile_in, tile_out = (2 * width_in, 4 * rows_in), (2 * rows_out, 2 * width_out)
    g0 = call(
        lambda *refs: rotate_out_kernel(tin, *refs),
        shape(tile_out, bf16),
        (own_grads, grads_near, own_basis_out, basis_out_far),
        [pltpu.VMEM((depth, 2 * width_out), bf16)],
        flops=8 * rows_out * width_out * depth,
    )
    acts_near, _ = lax.optimization_barrier((acts_near, g0))
    acts_near_core = hid(acts_near, 1)
    weights = call(join_kernel, shape((depth, 2 * width_in), bf16), (own_basis_in, basis_far), flops=8000000000)
    t0 = call(
        rotate_in_kernel,
        shape(tile_in, bf16),
        (own_acts, acts_core, acts_near, acts_near_core, weights),
        flops=16 * rows_in * width_in * depth + 2000000000,
    )
    t1 = hid(t0, tok_in)
    t2 = hid(t0, col_in)
    g1 = inb(g0, tok_out)
    g2 = inb(g0, col_out)
    s0 = hid(t0, 1)
    s1 = hid(t1, 1)
    s2 = hid(t2, 1)
    t1_then = call(copy_kernel, shape(tile_in, bf16), (t1,), flops=4000000000)
    t3 = hid(t1_then, col_in)
    onward = []
    for h in range(n_hid):
        step = col_out if h % 2 == 0 else tok_out
        onward += [(i * n_hid + h, (i ^ step) * n_hid + h) for i in range(n_inb)]
    g1_then, g2_then, _ = lax.optimization_barrier((g1, g2, t0))
    picked = call(lambda *refs: pick_kernel(is_first_core, *refs), shape(tile_out, bf16), (g1_then, g2_then), flops=0)
    g3 = lax.ppermute(picked, ("inb", "hid"), onward)

    half_rows, half_columns, half_tokens = 2 * tile_in[0], tile_out[1], tile_out[0]
    columns, half_out = 2 * half_columns, (half_rows, 2 * half_columns)
    top, grad, fisher, _, right, _ = call(
        early_kernel,
        [
            shape(half_out, bf16),
            shape(half_out, f32),
            shape(half_out, f32),
            shape((half_rows, 2 * half_tokens), bf16),
            shape((2 * half_tokens, columns), bf16),
            shape((half_rows, half_tokens), bf16),
        ],
        (t0, t1, t2, s0, s1, s2, g0, g1, g2, g3),
        flops=2000000000,
    )
    t3, top = lax.optimization_barrier((t3, top))
    t3 = call(copy_kernel, shape(tile_in, bf16), (t3,), flops=4000000000)
    s3 = hid(t3, 1)
    return call(
        late_kernel,
        shape((activations.shape[2], out_grads.shape[2]), bf16),
        (top, grad, fisher, right, t3, s3),
        [pltpu.VMEM(half_out, bf16), pltpu.SemaphoreType.DMA((8,))],
        flops=4 * half_rows * half_columns * half_tokens,
        out_space=anywhere,
    )


def solution(mesh):
    n_inb, n_hid = mesh.shape["inb"], mesh.shape["hid"]
    two_by_two = n_inb == 2 * 2 and n_hid == 2 * n_inb
    body = (lambda *a: paired(n_inb, n_hid, *a)) if two_by_two else gathered
    return jax.shard_map(
        body,
        mesh=mesh,
        in_specs=(P(None, "hid", "inb"), P(None, "inb", "hid"), P("inb", "hid"), P("hid", "inb")),
        out_specs=P("inb", "hid"),
        check_vma=False,
    )
```

```python
import functools

import jax
import jax.numpy as jnp
from jax import lax
from jax.experimental import pallas as pl
from jax.experimental.pallas import tpu as pltpu
from jax.sharding import PartitionSpec as P

damping = 0.1


def square_round(values):
    widened = values.astype(jnp.float32)
    return (widened * widened).astype(jnp.bfloat16)


def contract_tokens(left_side, right_side):
    return lax.dot_general(
        left_side, right_side, (((0, 1), (0, 1)), ((), ())), preferred_element_type=jnp.float32
    )


def gathered(activations, out_grads, basis_in, basis_out):
    width_block = basis_in.shape[0]
    grads_flat = out_grads.reshape(-1, width_block)
    grads_rot = (
        jnp.dot(
            grads_flat,
            lax.all_gather(basis_out, "inb", axis=1, tiled=True),
            preferred_element_type=jnp.float32,
        )
        .astype(jnp.bfloat16)
        .reshape(out_grads.shape)
    )
    basis_whole = lax.all_gather(basis_in, "hid", axis=1, tiled=True)
    grads_full = lax.all_gather(grads_rot, "inb", axis=1, tiled=True)
    grads_squared = square_round(grads_full)
    plain_rows = lax.all_gather(activations, "hid", axis=1, tiled=True)
    rotated = (
        jnp.dot(
            plain_rows.reshape(-1, width_block), basis_whole, preferred_element_type=jnp.float32
        )
        .astype(jnp.bfloat16)
        .reshape(plain_rows.shape)
    )
    grad_sum = contract_tokens(rotated, grads_full)
    fisher_sum = contract_tokens(square_round(rotated), grads_squared)
    return (grad_sum / (fisher_sum + damping)).astype(jnp.bfloat16)


def swap(values, axis, count, distance):
    return lax.ppermute(values, axis, [(i, i ^ distance) for i in range(count)])


def rows_of(index, size):
    return pl.ds(pl.multiple_of(index * size, size), size)


def hid_digits():
    index = lax.axis_index("hid")
    return index // 4, lax.rem(index // 2, 2), lax.rem(index, 2)


def inb_digits():
    index = lax.axis_index("inb")
    return index // 2, lax.rem(index, 2)


def other_tokens():
    return lax.rem(hid_digits()[1] + inb_digits()[1], 2)


def dot(a, b):
    return jnp.dot(a, b, preferred_element_type=jnp.float32)


def fetch_kernel(*refs):
    count = len(refs) // 2
    copies = [pltpu.make_async_copy(refs[k], refs[count + k], refs[-1].at[k]) for k in range(count)]
    for copy in copies:
        copy.start()
    for copy in copies:
        copy.wait()


def rotate_out_kernel(run, own_ref, near_ref, basis_ref, far_ref, tile_ref, weights):
    tok, col = inb_digits()
    micro, tokens, depth = own_ref.shape
    width = basis_ref.shape[1]
    weights[:, rows_of(col, width)] = basis_ref[...]
    weights[:, rows_of(1 - col, width)] = far_ref[...]
    for grads_ref, place in ((own_ref, tok), (near_ref, 1 - tok)):
        part = dot(grads_ref[...].reshape(micro * tokens, depth), weights[...]).astype(jnp.bfloat16)
        for m in range(micro):
            for k in range(tokens // run):
                here = m * tokens + k * run
                row = place * (micro * tokens) + (k * micro + m) * run
                tile_ref[pl.ds(pl.multiple_of(row, run), run), :] = part[here : here + run]


def join_kernel(basis_ref, far_ref, weights):
    col = hid_digits()[1]
    width = basis_ref.shape[1]
    weights[:, rows_of(col, width)] = basis_ref[...]
    weights[:, rows_of(1 - col, width)] = far_ref[...]


def rotate_in_kernel(own_ref, core_ref, near_ref, near_core_ref, weights, tile_ref):
    tok, _, core = hid_digits()
    micro, tokens, depth = own_ref.shape
    for acts_ref, place in (
        (own_ref, 2 * tok + core),
        (core_ref, 2 * tok + 1 - core),
        (near_ref, 2 * (1 - tok) + core),
        (near_core_ref, 2 * (1 - tok) + 1 - core),
    ):
        acts = acts_ref[...].reshape(micro * tokens, depth)
        part = dot(acts, weights[...])
        tile_ref[:, rows_of(place, micro * tokens)] = part.astype(jnp.bfloat16).T


def pick_kernel(which, a_ref, b_ref, out_ref):
    first = which()

    @pl.when(first)
    def _():
        out_ref[...] = a_ref[...]

    @pl.when(jnp.logical_not(first))
    def _():
        out_ref[...] = b_ref[...]


def copy_kernel(a_ref, out_ref):
    out_ref[...] = a_ref[...]


def is_first_core():
    return hid_digits()[2] == 0


def squared(values):
    return values * values


def ratio(g, f):
    return (g / (f + damping)).astype(jnp.bfloat16)


def send_rows(source, out_ref, row_tok, core, number, columns, sems):
    size = source.shape[0] // 2
    copies = []
    for k in range(2):
        here = rows_of(4 * row_tok + 2 * k + core, size)
        copies.append(
            pltpu.make_async_copy(source.at[k * size : (k + 1) * size, columns], out_ref.at[here, columns], sems.at[number + k])
        )
    for copy in copies:
        copy.start()
    return copies


def early_kernel(t0, t1, t2, s0, s1, s2, g0, g1, g2, g3, out_ref, grad, fisher, left, right, side, top, sems):
    out_tok, _ = inb_digits()
    other = other_tokens()
    size, span = t0.shape
    width = g0.shape[1]
    for k, (t, t_far, t_side) in enumerate(((t0, t2, t1), (s0, s2, s1))):
        at = slice(k * size, (k + 1) * size)
        left[at, :span] = t[...]
        left[at, span:] = t_far[...]
        side[at] = t_side[...]
    for half, column, tile in ((other, out_tok, g0), (1 - other, out_tok, g2), (other, 1 - out_tok, g1), (1 - other, 1 - out_tok, g3)):
        right[rows_of(half, span), rows_of(column, width)] = tile[...]
    tok, _, core = hid_digits()
    cores, copies = (core, 1 - core), []
    for c in range(2):
        columns = slice(c * width, (c + 1) * width)
        whole = right[:, columns]
        whole_squared = squared(whole)
        for k in range(2):
            at = slice(k * size, (k + 1) * size)
            rows = left[at]
            top[at, columns] = ratio(dot(rows, whole), dot(squared(rows), whole_squared))
            copies += send_rows(top.at[at, :], out_ref, tok, cores[k], 4 * c + 2 * k, columns, sems)
            rows = side[at]
            grad[at, columns] = dot(rows, whole[:span])
            fisher[at, columns] = dot(squared(rows), whole_squared[:span])
    for copy in copies:
        copy.wait()


def rest_kernel(part, out_in, grad, fisher, right, t, out_ref, done, sems):
    tok, _, core = hid_digits()
    size, span = t.shape
    width = right.shape[1] // 2
    at = slice(part * size, (part + 1) * size)
    rows = t[...]
    rows_squared = squared(rows)
    copies = []
    for c in range(2):
        columns = slice(c * width, (c + 1) * width)
        beside = right[span:, columns]
        g = grad[at, columns] + dot(rows, beside)
        f = fisher[at, columns] + dot(rows_squared, squared(beside))
        done[:, columns] = ratio(g, f)
        copies += send_rows(done, out_ref, 1 - tok, core if part == 0 else 1 - core, 2 * c, columns, sems)
    for copy in copies:
        copy.wait()


def paired(n_inb, n_hid, activations, out_grads, basis_in, basis_out):
    vmem, anywhere = pl.BlockSpec(memory_space=pltpu.VMEM), pl.BlockSpec(memory_space=pl.ANY)
    params = pltpu.CompilerParams(vmem_limit_bytes=24 * 1024 * 1024)
    bf16, f32 = jnp.bfloat16, jnp.float32
    shape = jax.ShapeDtypeStruct

    def hid(values, distance):
        return swap(values, "hid", n_hid, distance)

    def inb(values, distance):
        return swap(values, "inb", n_inb, distance)

    tok_in, col_in = n_hid // 2, n_hid // 4
    tok_out, col_out = n_inb // 2, n_inb // 4

    def call(kernel, outs, operands, scratch=(), flops=0, space=vmem, out_specs=None):
        one = not isinstance(outs, list)
        return pl.pallas_call(
            kernel,
            out_shape=outs,
            in_specs=[space] * len(operands),
            out_specs=out_specs or (vmem if one else [vmem] * len(outs)),
            scratch_shapes=scratch,
            compiler_params=params,
            cost_estimate=pl.CostEstimate(flops=flops, bytes_accessed=0, transcendentals=0),
        )(*operands)

    acts_near = hid(activations, tok_in)
    basis_far = hid(basis_in, col_in)
    grads_near = inb(out_grads, tok_out)
    basis_out_far = inb(basis_out, col_out)
    acts_core = hid(activations, 1)

    own = (out_grads, basis_out, activations, basis_in)
    own_grads, own_basis_out, own_acts, own_basis_in = call(
        fetch_kernel,
        [shape(v.shape, v.dtype) for v in own],
        own,
        [pltpu.SemaphoreType.DMA((len(own),))],
        space=anywhere,
    )

    micro, tin, depth = activations.shape
    tout = out_grads.shape[1]
    rows_out, width_out = micro * tout, basis_out.shape[1]
    rows_in, width_in = micro * tin, basis_in.shape[1]
    tile_in, tile_out = (2 * width_in, 4 * rows_in), (2 * rows_out, 2 * width_out)
    g0 = call(
        lambda *refs: rotate_out_kernel(tin, *refs),
        shape(tile_out, bf16),
        (own_grads, grads_near, own_basis_out, basis_out_far),
        [pltpu.VMEM((depth, 2 * width_out), bf16)],
        flops=8 * rows_out * width_out * depth,
    )
    acts_near, _ = lax.optimization_barrier((acts_near, g0))
    acts_near_core = hid(acts_near, 1)
    weights = call(join_kernel, shape((depth, 2 * width_in), bf16), (own_basis_in, basis_far), flops=8000000000)
    t0 = call(
        rotate_in_kernel,
        shape(tile_in, bf16),
        (own_acts, acts_core, acts_near, acts_near_core, weights),
        flops=16 * rows_in * width_in * depth + 2000000000,
    )
    t1 = hid(t0, tok_in)
    t2 = hid(t0, col_in)
    g1 = inb(g0, tok_out)
    g2 = inb(g0, col_out)
    s0 = hid(t0, 1)
    s1 = hid(t1, 1)
    s2 = hid(t2, 1)
    t1_then = call(copy_kernel, shape(tile_in, bf16), (t1,), flops=4000000000)
    t3 = hid(t1_then, col_in)
    onward = []
    for h in range(n_hid):
        step = col_out if h % 2 == 0 else tok_out
        onward += [(i * n_hid + h, (i ^ step) * n_hid + h) for i in range(n_inb)]
    g1_then, g2_then, _ = lax.optimization_barrier((g1, g2, t0))
    picked = call(lambda *refs: pick_kernel(is_first_core, *refs), shape(tile_out, bf16), (g1_then, g2_then), flops=0)
    g3 = lax.ppermute(picked, ("inb", "hid"), onward)

    half_rows, half_columns, half_tokens = 2 * tile_in[0], tile_out[1], tile_out[0]
    columns, half_out = 2 * half_columns, (half_rows, 2 * half_columns)
    out, grad, fisher, _, right, _ = call(
        early_kernel,
        [
            shape((activations.shape[2], out_grads.shape[2]), bf16),
            shape(half_out, f32),
            shape(half_out, f32),
            shape((half_rows, 2 * half_tokens), bf16),
            shape((2 * half_tokens, columns), bf16),
            shape((half_rows, half_tokens), bf16),
        ],
        (t0, t1, t2, s0, s1, s2, g0, g1, g2, g3),
        [pltpu.VMEM(half_out, bf16), pltpu.SemaphoreType.DMA((8,))],
        flops=2000000000,
        out_specs=[anywhere] + [vmem] * 5,
    )
    t3, grad = lax.optimization_barrier((t3, grad))
    t3 = call(copy_kernel, shape(tile_in, bf16), (t3,), flops=4000000000)
    s3 = hid(t3, 1)
    for part, tile in enumerate((t3, s3)):
        out = pl.pallas_call(
            functools.partial(rest_kernel, part),
            out_shape=shape(out.shape, bf16),
            in_specs=[anywhere] + [vmem] * 4,
            out_specs=anywhere,
            scratch_shapes=[pltpu.VMEM((tile_in[0], columns), bf16), pltpu.SemaphoreType.DMA((4,))],
            input_output_aliases={0: 0},
            compiler_params=params,
            cost_estimate=pl.CostEstimate(flops=500000000, bytes_accessed=0, transcendentals=0),
        )(out, grad, fisher, right, tile)
    return out


def solution(mesh):
    n_inb, n_hid = mesh.shape["inb"], mesh.shape["hid"]
    two_by_two = n_inb == 2 * 2 and n_hid == 2 * n_inb
    body = (lambda *a: paired(n_inb, n_hid, *a)) if two_by_two else gathered
    return jax.shard_map(
        body,
        mesh=mesh,
        in_specs=(P(None, "hid", "inb"), P(None, "inb", "hid"), P("inb", "hid"), P("hid", "inb")),
        out_specs=P("inb", "hid"),
        check_vma=False,
    )
```

```python
import jax
import jax.numpy as jnp
from jax import lax
from jax.experimental import pallas as pl
from jax.experimental.pallas import tpu as pltpu
from jax.sharding import PartitionSpec as P

damping = 0.1


def square_round(values):
    widened = values.astype(jnp.float32)
    return (widened * widened).astype(jnp.bfloat16)


def contract_tokens(left_side, right_side):
    return lax.dot_general(
        left_side, right_side, (((0, 1), (0, 1)), ((), ())), preferred_element_type=jnp.float32
    )


def gathered(activations, out_grads, basis_in, basis_out):
    width_block = basis_in.shape[0]
    grads_flat = out_grads.reshape(-1, width_block)
    grads_rot = (
        jnp.dot(
            grads_flat,
            lax.all_gather(basis_out, "inb", axis=1, tiled=True),
            preferred_element_type=jnp.float32,
        )
        .astype(jnp.bfloat16)
        .reshape(out_grads.shape)
    )
    basis_whole = lax.all_gather(basis_in, "hid", axis=1, tiled=True)
    grads_full = lax.all_gather(grads_rot, "inb", axis=1, tiled=True)
    grads_squared = square_round(grads_full)
    plain_rows = lax.all_gather(activations, "hid", axis=1, tiled=True)
    rotated = (
        jnp.dot(
            plain_rows.reshape(-1, width_block), basis_whole, preferred_element_type=jnp.float32
        )
        .astype(jnp.bfloat16)
        .reshape(plain_rows.shape)
    )
    grad_sum = contract_tokens(rotated, grads_full)
    fisher_sum = contract_tokens(square_round(rotated), grads_squared)
    return (grad_sum / (fisher_sum + damping)).astype(jnp.bfloat16)


def swap(values, axis, count, distance):
    return lax.ppermute(values, axis, [(i, i ^ distance) for i in range(count)])


def rows_of(index, size):
    return pl.ds(pl.multiple_of(index * size, size), size)


def hid_digits():
    index = lax.axis_index("hid")
    return index // 4, lax.rem(index // 2, 2), lax.rem(index, 2)


def inb_digits():
    index = lax.axis_index("inb")
    return index // 2, lax.rem(index, 2)


def other_tokens():
    return lax.rem(hid_digits()[1] + inb_digits()[1], 2)


def dot(a, b):
    return jnp.dot(a, b, preferred_element_type=jnp.float32)


def fetch_kernel(*refs):
    count = len(refs) // 2
    copies = [pltpu.make_async_copy(refs[k], refs[count + k], refs[-1].at[k]) for k in range(count)]
    for copy in copies:
        copy.start()
    for copy in copies:
        copy.wait()


def rotate_out_kernel(run, own_ref, near_ref, basis_ref, far_ref, tile_ref, weights):
    tok, col = inb_digits()
    micro, tokens, depth = own_ref.shape
    width = basis_ref.shape[1]
    weights[:, rows_of(col, width)] = basis_ref[...]
    weights[:, rows_of(1 - col, width)] = far_ref[...]
    for grads_ref, place in ((own_ref, tok), (near_ref, 1 - tok)):
        part = dot(grads_ref[...].reshape(micro * tokens, depth), weights[...]).astype(jnp.bfloat16)
        for m in range(micro):
            for k in range(tokens // run):
                here = m * tokens + k * run
                row = place * (micro * tokens) + (k * micro + m) * run
                tile_ref[pl.ds(pl.multiple_of(row, run), run), :] = part[here : here + run]


def join_kernel(basis_ref, far_ref, weights):
    col = hid_digits()[1]
    width = basis_ref.shape[1]
    weights[:, rows_of(col, width)] = basis_ref[...]
    weights[:, rows_of(1 - col, width)] = far_ref[...]


def rotate_in_kernel(own_ref, core_ref, near_ref, near_core_ref, weights, tile_ref):
    tok, _, core = hid_digits()
    micro, tokens, depth = own_ref.shape
    for acts_ref, place in (
        (own_ref, 2 * tok + core),
        (core_ref, 2 * tok + 1 - core),
        (near_ref, 2 * (1 - tok) + core),
        (near_core_ref, 2 * (1 - tok) + 1 - core),
    ):
        acts = acts_ref[...].reshape(micro * tokens, depth)
        part = dot(acts, weights[...])
        tile_ref[:, rows_of(place, micro * tokens)] = part.astype(jnp.bfloat16).T


def pick_kernel(which, a_ref, b_ref, out_ref):
    first = which()

    @pl.when(first)
    def _():
        out_ref[...] = a_ref[...]

    @pl.when(jnp.logical_not(first))
    def _():
        out_ref[...] = b_ref[...]


def copy_kernel(a_ref, out_ref):
    out_ref[...] = a_ref[...]


def is_first_core():
    return hid_digits()[2] == 0


def squared(values):
    return values * values


def ratio(g, f):
    return (g / (f + damping)).astype(jnp.bfloat16)


def send_rows(source, out_ref, row_tok, core, number, columns, sems):
    size = source.shape[0] // 2
    copies = []
    for k in range(2):
        here = rows_of(4 * row_tok + 2 * k + core, size)
        copies.append(
            pltpu.make_async_copy(source.at[k * size : (k + 1) * size, columns], out_ref.at[here, columns], sems.at[number + k])
        )
    for copy in copies:
        copy.start()
    return copies


def early_kernel(t0, t2, s0, s1, s2, g0, g1, g2, g3, out_ref, grad, fisher, left, right, top, sems):
    out_tok, _ = inb_digits()
    other = other_tokens()
    size, span = t0.shape
    width = g0.shape[1]
    for k, (t, t_far) in enumerate(((t0, t2), (s0, s2))):
        at = slice(k * size, (k + 1) * size)
        left[at, :span] = t[...]
        left[at, span:] = t_far[...]
    for half, column, tile in ((other, out_tok, g0), (1 - other, out_tok, g2), (other, 1 - out_tok, g1), (1 - other, 1 - out_tok, g3)):
        right[rows_of(half, span), rows_of(column, width)] = tile[...]
    tok, _, core = hid_digits()
    cores, copies = (core, 1 - core), []
    for c in range(2):
        columns = slice(c * width, (c + 1) * width)
        whole = right[:, columns]
        whole_squared = squared(whole)
        for k in range(2):
            at = slice(k * size, (k + 1) * size)
            rows = left[at]
            top[at, columns] = ratio(dot(rows, whole), dot(squared(rows), whole_squared))
            copies += send_rows(top.at[at, :], out_ref, tok, cores[k], 4 * c + 2 * k, columns, sems)
        rows = s1[...]
        grad[:, columns] = dot(rows, whole[:span])
        fisher[:, columns] = dot(squared(rows), whole_squared[:span])
    for copy in copies:
        copy.wait()


def middle_kernel(right, t1, t3, done, rows):
    span = t1.shape[1]
    width = right.shape[1] // 2
    rows[:, :span] = t1[...]
    rows[:, span:] = t3[...]
    values = rows[...]
    values_squared = squared(values)
    for c in range(2):
        columns = slice(c * width, (c + 1) * width)
        beside = right[:, columns]
        done[:, columns] = ratio(dot(values, beside), dot(values_squared, squared(beside)))


def late_kernel(out_in, first, grad, fisher, right, s, out_ref, done, sems):
    tok, _, core = hid_digits()
    span, width = s.shape[1], right.shape[1] // 2
    copies = send_rows(first, out_ref, 1 - tok, core, 0, slice(0, done.shape[1]), sems)
    rows = s[...]
    rows_squared = squared(rows)
    for c in range(2):
        columns = slice(c * width, (c + 1) * width)
        beside = right[span:, columns]
        g = grad[:, columns] + dot(rows, beside)
        f = fisher[:, columns] + dot(rows_squared, squared(beside))
        done[:, columns] = ratio(g, f)
        copies += send_rows(done, out_ref, 1 - tok, 1 - core, 2 + 2 * c, columns, sems)
    for copy in copies:
        copy.wait()


def paired(n_inb, n_hid, activations, out_grads, basis_in, basis_out):
    vmem, anywhere = pl.BlockSpec(memory_space=pltpu.VMEM), pl.BlockSpec(memory_space=pl.ANY)
    params = pltpu.CompilerParams(vmem_limit_bytes=24 * 1024 * 1024)
    bf16, f32 = jnp.bfloat16, jnp.float32
    shape = jax.ShapeDtypeStruct

    def hid(values, distance):
        return swap(values, "hid", n_hid, distance)

    def inb(values, distance):
        return swap(values, "inb", n_inb, distance)

    tok_in, col_in = n_hid // 2, n_hid // 4
    tok_out, col_out = n_inb // 2, n_inb // 4

    def call(kernel, outs, operands, scratch=(), flops=0, space=vmem, out_specs=None):
        one = not isinstance(outs, list)
        return pl.pallas_call(
            kernel,
            out_shape=outs,
            in_specs=[space] * len(operands),
            out_specs=out_specs or (vmem if one else [vmem] * len(outs)),
            scratch_shapes=scratch,
            compiler_params=params,
            cost_estimate=pl.CostEstimate(flops=flops, bytes_accessed=0, transcendentals=0),
        )(*operands)

    acts_near = hid(activations, tok_in)
    basis_far = hid(basis_in, col_in)
    grads_near = inb(out_grads, tok_out)
    basis_out_far = inb(basis_out, col_out)
    acts_core = hid(activations, 1)

    own = (out_grads, basis_out, activations, basis_in)
    own_grads, own_basis_out, own_acts, own_basis_in = call(
        fetch_kernel,
        [shape(v.shape, v.dtype) for v in own],
        own,
        [pltpu.SemaphoreType.DMA((len(own),))],
        space=anywhere,
    )

    micro, tin, depth = activations.shape
    tout = out_grads.shape[1]
    rows_out, width_out = micro * tout, basis_out.shape[1]
    rows_in, width_in = micro * tin, basis_in.shape[1]
    tile_in, tile_out = (2 * width_in, 4 * rows_in), (2 * rows_out, 2 * width_out)
    g0 = call(
        lambda *refs: rotate_out_kernel(tin, *refs),
        shape(tile_out, bf16),
        (own_grads, grads_near, own_basis_out, basis_out_far),
        [pltpu.VMEM((depth, 2 * width_out), bf16)],
        flops=8 * rows_out * width_out * depth,
    )
    acts_near, _ = lax.optimization_barrier((acts_near, g0))
    acts_near_core = hid(acts_near, 1)
    weights = call(join_kernel, shape((depth, 2 * width_in), bf16), (own_basis_in, basis_far), flops=8000000000)
    t0 = call(
        rotate_in_kernel,
        shape(tile_in, bf16),
        (own_acts, acts_core, acts_near, acts_near_core, weights),
        flops=16 * rows_in * width_in * depth + 2000000000,
    )
    t1 = hid(t0, tok_in)
    t2 = hid(t0, col_in)
    g1 = inb(g0, tok_out)
    g2 = inb(g0, col_out)
    s0 = hid(t0, 1)
    t1_then = call(copy_kernel, shape(tile_in, bf16), (t1,), flops=4000000000)
    t3 = hid(t1_then, col_in)
    s1 = hid(t1_then, 1)
    t2_then, _ = lax.optimization_barrier((t2, t1_then))
    s2 = hid(t2_then, 1)
    onward = []
    for h in range(n_hid):
        step = col_out if h % 2 == 0 else tok_out
        onward += [(i * n_hid + h, (i ^ step) * n_hid + h) for i in range(n_inb)]
    g1_then, g2_then, _ = lax.optimization_barrier((g1, g2, t0))
    picked = call(lambda *refs: pick_kernel(is_first_core, *refs), shape(tile_out, bf16), (g1_then, g2_then), flops=0)
    g3 = lax.ppermute(picked, ("inb", "hid"), onward)

    half_rows, half_columns, half_tokens = 2 * tile_in[0], tile_out[1], tile_out[0]
    columns, half_out = 2 * half_columns, (half_rows, 2 * half_columns)
    part_rows = (tile_in[0], columns)
    out, grad, fisher, _, right = call(
        early_kernel,
        [
            shape((activations.shape[2], out_grads.shape[2]), bf16),
            shape(part_rows, f32),
            shape(part_rows, f32),
            shape((half_rows, 2 * half_tokens), bf16),
            shape((2 * half_tokens, columns), bf16),
        ],
        (t0, t2_then, s0, s1, s2, g0, g1, g2, g3),
        [pltpu.VMEM(half_out, bf16), pltpu.SemaphoreType.DMA((8,))],
        flops=0,
        out_specs=[anywhere] + [vmem] * 4,
    )
    t3, grad = lax.optimization_barrier((t3, grad))
    t3 = call(copy_kernel, shape(tile_in, bf16), (t3,), flops=4000000000)
    s3 = hid(t3, 1)
    first = call(
        middle_kernel,
        shape(part_rows, bf16),
        (right, t1_then, t3),
        [pltpu.VMEM((tile_in[0], 2 * half_tokens), bf16)],
        flops=500000000,
    )
    return pl.pallas_call(
        late_kernel,
        out_shape=shape(out.shape, bf16),
        in_specs=[anywhere] + [vmem] * 5,
        out_specs=anywhere,
        scratch_shapes=[pltpu.VMEM(part_rows, bf16), pltpu.SemaphoreType.DMA((6,))],
        input_output_aliases={0: 0},
        compiler_params=params,
    )(out, first, grad, fisher, right, s3)


def solution(mesh):
    n_inb, n_hid = mesh.shape["inb"], mesh.shape["hid"]
    two_by_two = n_inb == 2 * 2 and n_hid == 2 * n_inb
    body = (lambda *a: paired(n_inb, n_hid, *a)) if two_by_two else gathered
    return jax.shard_map(
        body,
        mesh=mesh,
        in_specs=(P(None, "hid", "inb"), P(None, "inb", "hid"), P("inb", "hid"), P("hid", "inb")),
        out_specs=P("inb", "hid"),
        check_vma=False,
    )
```

```python
import jax
import jax.numpy as jnp
from jax import lax
from jax.experimental import pallas as pl
from jax.experimental.pallas import tpu as pltpu
from jax.sharding import PartitionSpec as P

damping = 0.1


def square_round(values):
    widened = values.astype(jnp.float32)
    return (widened * widened).astype(jnp.bfloat16)


def contract_tokens(left_side, right_side):
    return lax.dot_general(
        left_side, right_side, (((0, 1), (0, 1)), ((), ())), preferred_element_type=jnp.float32
    )


def gathered(activations, out_grads, basis_in, basis_out):
    width_block = basis_in.shape[0]
    grads_flat = out_grads.reshape(-1, width_block)
    grads_rot = (
        jnp.dot(
            grads_flat,
            lax.all_gather(basis_out, "inb", axis=1, tiled=True),
            preferred_element_type=jnp.float32,
        )
        .astype(jnp.bfloat16)
        .reshape(out_grads.shape)
    )
    basis_whole = lax.all_gather(basis_in, "hid", axis=1, tiled=True)
    grads_full = lax.all_gather(grads_rot, "inb", axis=1, tiled=True)
    grads_squared = square_round(grads_full)
    plain_rows = lax.all_gather(activations, "hid", axis=1, tiled=True)
    rotated = (
        jnp.dot(
            plain_rows.reshape(-1, width_block), basis_whole, preferred_element_type=jnp.float32
        )
        .astype(jnp.bfloat16)
        .reshape(plain_rows.shape)
    )
    grad_sum = contract_tokens(rotated, grads_full)
    fisher_sum = contract_tokens(square_round(rotated), grads_squared)
    return (grad_sum / (fisher_sum + damping)).astype(jnp.bfloat16)


def swap(values, axis, count, distance):
    return lax.ppermute(values, axis, [(i, i ^ distance) for i in range(count)])


def rows_of(index, size):
    return pl.ds(pl.multiple_of(index * size, size), size)


def hid_digits():
    index = lax.axis_index("hid")
    return index // 4, lax.rem(index // 2, 2), lax.rem(index, 2)


def inb_digits():
    index = lax.axis_index("inb")
    return index // 2, lax.rem(index, 2)


def other_tokens():
    return lax.rem(hid_digits()[1] + inb_digits()[1], 2)


def dot(a, b):
    return jnp.dot(a, b, preferred_element_type=jnp.float32)


def fetch_kernel(*refs):
    count = len(refs) // 2
    copies = [pltpu.make_async_copy(refs[k], refs[count + k], refs[-1].at[k]) for k in range(count)]
    for copy in copies:
        copy.start()
    for copy in copies:
        copy.wait()


def rotate_out_kernel(run, own_ref, near_ref, basis_ref, far_ref, tile_ref, weights):
    tok, col = inb_digits()
    micro, tokens, depth = own_ref.shape
    width = basis_ref.shape[1]
    weights[:, rows_of(col, width)] = basis_ref[...]
    weights[:, rows_of(1 - col, width)] = far_ref[...]
    for grads_ref, place in ((own_ref, tok), (near_ref, 1 - tok)):
        part = dot(grads_ref[...].reshape(micro * tokens, depth), weights[...]).astype(jnp.bfloat16)
        for m in range(micro):
            for k in range(tokens // run):
                here = m * tokens + k * run
                row = place * (micro * tokens) + (k * micro + m) * run
                tile_ref[pl.ds(pl.multiple_of(row, run), run), :] = part[here : here + run]


def join_kernel(basis_ref, far_ref, weights):
    col = hid_digits()[1]
    width = basis_ref.shape[1]
    weights[:, rows_of(col, width)] = basis_ref[...]
    weights[:, rows_of(1 - col, width)] = far_ref[...]


def rotate_in_kernel(own_ref, core_ref, near_ref, near_core_ref, weights, tile_ref):
    tok, _, core = hid_digits()
    micro, tokens, depth = own_ref.shape
    for acts_ref, place in (
        (own_ref, 2 * tok + core),
        (core_ref, 2 * tok + 1 - core),
        (near_ref, 2 * (1 - tok) + core),
        (near_core_ref, 2 * (1 - tok) + 1 - core),
    ):
        acts = acts_ref[...].reshape(micro * tokens, depth)
        part = dot(acts, weights[...])
        tile_ref[:, rows_of(place, micro * tokens)] = part.astype(jnp.bfloat16).T


def pick_kernel(which, a_ref, b_ref, out_ref):
    first = which()

    @pl.when(first)
    def _():
        out_ref[...] = a_ref[...]

    @pl.when(jnp.logical_not(first))
    def _():
        out_ref[...] = b_ref[...]


def copy_kernel(a_ref, out_ref):
    out_ref[...] = a_ref[...]


def is_first_core():
    return hid_digits()[2] == 0


def squared(values):
    return values * values


def ratio(g, f):
    return (g / (f + damping)).astype(jnp.bfloat16)


def send_rows(source, out_ref, row_tok, core, number, columns, sems):
    size = source.shape[0] // 2
    copies = []
    for k in range(2):
        here = rows_of(4 * row_tok + 2 * k + core, size)
        copies.append(
            pltpu.make_async_copy(source.at[k * size : (k + 1) * size, columns], out_ref.at[here, columns], sems.at[number + k])
        )
    for copy in copies:
        copy.start()
    return copies


def early_kernel(t0, t2, s0, s1, s2, g0, g1, g2, g3, out_ref, grad, fisher, left, right, top, sems):
    out_tok, _ = inb_digits()
    other = other_tokens()
    size, span = t0.shape
    width = g0.shape[1]
    for k, (t, t_far) in enumerate(((t0, t2), (s0, s2))):
        at = slice(k * size, (k + 1) * size)
        left[at, :span] = t[...]
        left[at, span:] = t_far[...]
    for half, column, tile in ((other, out_tok, g0), (1 - other, out_tok, g2), (other, 1 - out_tok, g1), (1 - other, 1 - out_tok, g3)):
        right[rows_of(half, span), rows_of(column, width)] = tile[...]
    tok, _, core = hid_digits()
    cores, copies = (core, 1 - core), []
    for c in range(2):
        columns = slice(c * width, (c + 1) * width)
        whole = right[:, columns]
        whole_squared = squared(whole)
        for k in range(2):
            at = slice(k * size, (k + 1) * size)
            rows = left[at]
            top[at, columns] = ratio(dot(rows, whole), dot(squared(rows), whole_squared))
            copies += send_rows(top.at[at, :], out_ref, tok, cores[k], 4 * c + 2 * k, columns, sems)
        rows = s1[...]
        grad[:, columns] = dot(rows, whole[:span])
        fisher[:, columns] = dot(squared(rows), whole_squared[:span])
    for copy in copies:
        copy.wait()


def middle_kernel(right, t1, t3, done, rows):
    span = t1.shape[1]
    width = right.shape[1] // 2
    rows[:, :span] = t1[...]
    rows[:, span:] = t3[...]
    values = rows[...]
    values_squared = squared(values)
    for c in range(2):
        columns = slice(c * width, (c + 1) * width)
        beside = right[:, columns]
        done[:, columns] = ratio(dot(values, beside), dot(values_squared, squared(beside)))


def late_kernel(out_in, first, grad, fisher, right, s, out_ref, done, sems):
    tok, _, core = hid_digits()
    pieces = 4
    span, width = s.shape[1], right.shape[1] // pieces
    copies = send_rows(first, out_ref, 1 - tok, core, 0, slice(0, done.shape[1]), sems)
    rows = s[...]
    rows_squared = squared(rows)
    for c in range(pieces):
        columns = slice(c * width, (c + 1) * width)
        beside = right[span:, columns]
        g = grad[:, columns] + dot(rows, beside)
        f = fisher[:, columns] + dot(rows_squared, squared(beside))
        done[:, columns] = ratio(g, f)
        copies += send_rows(done, out_ref, 1 - tok, 1 - core, 2 + 2 * c, columns, sems)
    for copy in copies:
        copy.wait()


def paired(n_inb, n_hid, activations, out_grads, basis_in, basis_out):
    vmem, anywhere = pl.BlockSpec(memory_space=pltpu.VMEM), pl.BlockSpec(memory_space=pl.ANY)
    params = pltpu.CompilerParams(vmem_limit_bytes=24 * 1024 * 1024)
    bf16, f32 = jnp.bfloat16, jnp.float32
    shape = jax.ShapeDtypeStruct

    def hid(values, distance):
        return swap(values, "hid", n_hid, distance)

    def inb(values, distance):
        return swap(values, "inb", n_inb, distance)

    tok_in, col_in = n_hid // 2, n_hid // 4
    tok_out, col_out = n_inb // 2, n_inb // 4

    def call(kernel, outs, operands, scratch=(), flops=0, space=vmem, out_specs=None):
        one = not isinstance(outs, list)
        return pl.pallas_call(
            kernel,
            out_shape=outs,
            in_specs=[space] * len(operands),
            out_specs=out_specs or (vmem if one else [vmem] * len(outs)),
            scratch_shapes=scratch,
            compiler_params=params,
            cost_estimate=pl.CostEstimate(flops=flops, bytes_accessed=0, transcendentals=0),
        )(*operands)

    acts_near = hid(activations, tok_in)
    basis_far = hid(basis_in, col_in)
    grads_near = inb(out_grads, tok_out)
    basis_out_far = inb(basis_out, col_out)
    acts_core = hid(activations, 1)

    own = (out_grads, basis_out, activations, basis_in)
    own_grads, own_basis_out, own_acts, own_basis_in = call(
        fetch_kernel,
        [shape(v.shape, v.dtype) for v in own],
        own,
        [pltpu.SemaphoreType.DMA((len(own),))],
        space=anywhere,
    )

    micro, tin, depth = activations.shape
    tout = out_grads.shape[1]
    rows_out, width_out = micro * tout, basis_out.shape[1]
    rows_in, width_in = micro * tin, basis_in.shape[1]
    tile_in, tile_out = (2 * width_in, 4 * rows_in), (2 * rows_out, 2 * width_out)
    g0 = call(
        lambda *refs: rotate_out_kernel(tin, *refs),
        shape(tile_out, bf16),
        (own_grads, grads_near, own_basis_out, basis_out_far),
        [pltpu.VMEM((depth, 2 * width_out), bf16)],
        flops=8 * rows_out * width_out * depth,
    )
    acts_near, _ = lax.optimization_barrier((acts_near, g0))
    acts_near_core = hid(acts_near, 1)
    weights = call(join_kernel, shape((depth, 2 * width_in), bf16), (own_basis_in, basis_far), flops=8000000000)
    t0 = call(
        rotate_in_kernel,
        shape(tile_in, bf16),
        (own_acts, acts_core, acts_near, acts_near_core, weights),
        flops=16 * rows_in * width_in * depth + 2000000000,
    )
    t1 = hid(t0, tok_in)
    t2 = hid(t0, col_in)
    g1 = inb(g0, tok_out)
    g2 = inb(g0, col_out)
    s0 = hid(t0, 1)
    t1_then = call(copy_kernel, shape(tile_in, bf16), (t1,), flops=4000000000)
    t3 = hid(t1_then, col_in)
    s1 = hid(t1_then, 1)
    t2_then, _ = lax.optimization_barrier((t2, t1_then))
    s2 = hid(t2_then, 1)
    onward = []
    for h in range(n_hid):
        step = col_out if h % 2 == 0 else tok_out
        onward += [(i * n_hid + h, (i ^ step) * n_hid + h) for i in range(n_inb)]
    g1_then, g2_then, _ = lax.optimization_barrier((g1, g2, t0))
    picked = call(lambda *refs: pick_kernel(is_first_core, *refs), shape(tile_out, bf16), (g1_then, g2_then), flops=0)
    g3 = lax.ppermute(picked, ("inb", "hid"), onward)

    half_rows, half_columns, half_tokens = 2 * tile_in[0], tile_out[1], tile_out[0]
    columns, half_out = 2 * half_columns, (half_rows, 2 * half_columns)
    part_rows = (tile_in[0], columns)
    out, grad, fisher, _, right = call(
        early_kernel,
        [
            shape((activations.shape[2], out_grads.shape[2]), bf16),
            shape(part_rows, f32),
            shape(part_rows, f32),
            shape((half_rows, 2 * half_tokens), bf16),
            shape((2 * half_tokens, columns), bf16),
        ],
        (t0, t2_then, s0, s1, s2, g0, g1, g2, g3),
        [pltpu.VMEM(half_out, bf16), pltpu.SemaphoreType.DMA((8,))],
        flops=0,
        out_specs=[anywhere] + [vmem] * 4,
    )
    t3, grad = lax.optimization_barrier((t3, grad))
    t3 = call(copy_kernel, shape(tile_in, bf16), (t3,), flops=4000000000)
    s3 = hid(t3, 1)
    first = call(
        middle_kernel,
        shape(part_rows, bf16),
        (right, t1_then, t3),
        [pltpu.VMEM((tile_in[0], 2 * half_tokens), bf16)],
        flops=500000000,
    )
    return pl.pallas_call(
        late_kernel,
        out_shape=shape(out.shape, bf16),
        in_specs=[anywhere] + [vmem] * 5,
        out_specs=anywhere,
        scratch_shapes=[pltpu.VMEM(part_rows, bf16), pltpu.SemaphoreType.DMA((10,))],
        input_output_aliases={0: 0},
        compiler_params=params,
    )(out, first, grad, fisher, right, s3)


def solution(mesh):
    n_inb, n_hid = mesh.shape["inb"], mesh.shape["hid"]
    two_by_two = n_inb == 2 * 2 and n_hid == 2 * n_inb
    body = (lambda *a: paired(n_inb, n_hid, *a)) if two_by_two else gathered
    return jax.shard_map(
        body,
        mesh=mesh,
        in_specs=(P(None, "hid", "inb"), P(None, "inb", "hid"), P("inb", "hid"), P("hid", "inb")),
        out_specs=P("inb", "hid"),
        check_vma=False,
    )
```
